32 devices in a mesh: space: 16 (over z, y, x), tm: 2 (over core).
Axes of the slice: x: 2, y: 2, z: 4, core: 2. Of those that a mesh axis runs over, the one named last changes fastest.
Arguments:
- data: bfloat16 [32768, 2048], P('space', 'tm'), may hold values from -240 to 240
- row_factor: float32 [32768, 128], P('space'), may hold values from -1.8 to 1.8
- col_factor: float32 [2048, 128], P('tm'), may hold values from -1.8 to 1.8
Outputs:
- sparse: bfloat16 [32768, 2048], P('space', 'tm')
- row_out: float32 [32768, 128], P('space')
- col_out: float32 [2048, 128], P('tm')
The draws below stay inside these ranges and needn't reach their ends.
All inputs are finite; a program needn't handle non-finite values.
Results may differ from the reference program's by a relative error of at most 0.006.
Values sent between devices are 32-bit elements; how exact they have to be, the bound alone decides.
A program may use at most 64 MiB of HBM per device.

```python
import math
import jax
import jax.numpy as jnp
from jax import lax

RANK = 128
ROWS_DEV = 2048
ITERS = 2
ROWS = 32768
COLS = 2048


def row_profiles(key):
    keys = jax.random.split(jax.random.fold_in(key, 103), 3)
    place = jnp.arange(ROWS, dtype=jnp.float32) / ROWS
    upward = jax.random.uniform(keys[0], (), jnp.float32) < 0.5
    ramp = jnp.where(upward, place, 1.0 - place)
    waves = jax.random.randint(keys[1], (2,), 1, 4).astype(jnp.float32)
    phases = jax.random.uniform(keys[2], (2,), jnp.float32, 0.0, 2.0 * math.pi)
    signal_log = -2.0 + 2.2 * ramp + 0.3 * jnp.sin(2.0 * math.pi * waves[0] * place + phases[0])
    noise_log = -0.5 + 1.5 * ramp + 0.4 * jnp.sin(2.0 * math.pi * waves[1] * place + phases[1])
    return (signal_log, noise_log)


def shared_rows(key):
    signal_log, noise_log = row_profiles(key)
    keys = jax.random.split(jax.random.fold_in(key, 101), 2)
    rough = jax.random.uniform(keys[0], (ROWS, 1), jnp.float32, 0.8, 1.2)
    levels = jnp.exp(signal_log)[:, None] * rough
    base = jax.random.truncated_normal(keys[1], -3.0, 3.0, (ROWS, RANK), jnp.float32)
    return base * 0.3 * levels


def shared_cols(key, lowest):
    keys = jax.random.split(jax.random.fold_in(key, 102), 2)
    place = jnp.arange(COLS, dtype=jnp.float32) / (COLS - 1)
    trend = jnp.exp(math.log(lowest) + place * (math.log(1.6) - math.log(lowest)))[:, None]
    rough = jax.random.uniform(keys[0], (COLS, 1), jnp.float32, 0.8, 1.25)
    levels = trend * rough
    base = jax.random.truncated_normal(keys[1], -3.0, 3.0, (COLS, RANK), jnp.float32)
    return base * 0.3 * levels


def draw_row_factor(key, part):
    return shared_rows(key)


def draw_col_factor(key, part):
    lowest = 0.3
    return shared_cols(key, lowest)


def draw_data(key, part):
    lowest = 0.3
    upper = shared_rows(key)
    lower = shared_cols(key, lowest)
    signal_log, noise_log = row_profiles(key)
    key = jax.random.fold_in(key, 7)
    keys = jax.random.split(key, 3)
    row_noise = jnp.exp(noise_log)[:, None] * jax.random.uniform(keys[0], (ROWS, 1), jnp.float32, 0.7, 1.4)
    col_noise = jnp.exp(jax.random.uniform(keys[1], (1, COLS), jnp.float32, math.log(0.5), math.log(3.0)))
    base = jax.random.truncated_normal(keys[2], -4.0, 4.0, (ROWS, COLS), jnp.float32)
    weight = 3.0
    signal = jnp.dot(upper, lower.T, precision=lax.Precision.HIGHEST)
    values = weight * signal + base * row_noise * col_noise
    return jnp.clip(values, -240.0, 240.0).astype(jnp.bfloat16)


def setup_inputs(seed: int = 0) -> dict:
    streams_of = jax.random.split(jax.random.key(seed), 4)
    return {
        "data": draw_data(jax.random.fold_in(streams_of[3], 71), 0),
        "row_factor": draw_row_factor(jax.random.fold_in(streams_of[3], 71), 0),
        "col_factor": draw_col_factor(jax.random.fold_in(streams_of[3], 71), 0),
    }


threshold_scale = 1.0
step_scale = 8.0
ridge_weight = 64.0

def reference(data, row_factor, col_factor):
    upper = row_factor
    lower = col_factor
    sparse = jnp.zeros(data.shape, jnp.bfloat16)
    blocks = data.reshape(ROWS // ROWS_DEV, ROWS_DEV, COLS)
    for step in range(ITERS):
        upper_b = upper.astype(jnp.bfloat16)
        lower_b = lower.astype(jnp.bfloat16)
        up_blocks = upper_b.reshape(ROWS // ROWS_DEV, ROWS_DEV, RANK)

        def absolute(args):
            block, factor = args
            diff = block.astype(jnp.float32) - jnp.dot(factor, lower_b.T, preferred_element_type=jnp.float32)
            return jnp.sum(jnp.abs(diff))
        total = jnp.sum(lax.map(absolute, (blocks, up_blocks)))
        lam = threshold_scale * total / (ROWS * COLS)

        def second(args):
            block, factor = args
            diff = block.astype(jnp.float32) - jnp.dot(factor, lower_b.T, preferred_element_type=jnp.float32)
            part = (jnp.sign(diff) * jnp.maximum(jnp.abs(diff) - lam, 0.0)).astype(jnp.bfloat16)
            error = (part.astype(jnp.float32) - diff).astype(jnp.bfloat16)
            grad_rows = jnp.dot(error, lower_b, preferred_element_type=jnp.float32)
            grad_cols = lax.dot_general(error, factor, (((0,), (0,)), ((), ())), preferred_element_type=jnp.float32)
            return (part, grad_rows, grad_cols)
        parts, grad_rows, grad_cols = lax.map(second, (blocks, up_blocks))
        sparse = parts.reshape(ROWS, COLS)
        grad_u = grad_rows.reshape(ROWS, RANK)
        grad_v = lax.optimization_barrier(jnp.sum(grad_cols, axis=0))
        gram_u = jnp.dot(upper_b.T, upper_b, preferred_element_type=jnp.float32)
        gram_v = jnp.dot(lower_b.T, lower_b, preferred_element_type=jnp.float32)
        eta_u = step_scale / jnp.sqrt(jnp.sum(gram_v * gram_v))
        eta_v = step_scale / jnp.sqrt(jnp.sum(gram_u * gram_u))
        upper = upper - eta_u * (grad_u + ridge_weight * upper)
        lower = lower - eta_v * (grad_v + ridge_weight * lower)
    return (sparse, upper, lower)
```

```python
import functools

import jax
import jax.numpy as jnp
from jax import lax
from jax.experimental import pallas as pl
from jax.experimental.pallas import tpu as pltpu
from jax.sharding import PartitionSpec as P

ITERS = 2
MESH = pl.DeviceIdType.MESH
F32 = jnp.float32
BF16 = jnp.bfloat16

threshold_scale = 1.0
step_scale = 8.0
ridge_weight = 64.0


def dot(a, b):
    return jnp.dot(a, b, preferred_element_type=F32)


def dot_nt(a, b):
    return lax.dot_general(a, b, (((1,), (1,)), ((), ())), preferred_element_type=F32)


def total_of(x):
    return jnp.sum(jnp.sum(x, axis=0, keepdims=True), axis=1, keepdims=True)


def kernel(
    n, tm, G, H, count,
    data, u_in, v_in, sparse, u, v,
    diff, ub, ubt, vb, acc, gradt, tot_tm, tot_sp, gram_v, rows_sum, pay, plane_in, zsum, z_in, gathered,
    s_tot_tm, r_tot_tm, s_tot_sp, r_tot_sp, s_gram, r_gram, s_rows, r_rows,
    s_plane, r_plane, s_z, r_z, s_zg, r_zg, s_pg, r_pg,
):
    me = lax.axis_index("space")
    t = lax.axis_index("tm")
    h, g = me // G, me % G
    rows, cols = data.shape
    rank = u.shape[1]
    width = cols // G
    vr = width // H
    gr = rank // n
    blk = min(512, rows)

    barrier = pltpu.get_barrier_semaphore()
    for k in range(1, n):
        pl.semaphore_signal(barrier, inc=1, device_id=((me + k) % n, t), device_id_type=MESH)
    for k in range(1, tm):
        pl.semaphore_signal(barrier, inc=1, device_id=(me, (t + k) % tm), device_id_type=MESH)
    u[...] = u_in[...]
    v[...] = v_in[...]
    pl.semaphore_wait(barrier, n - 1 + tm - 1)

    def remote(src, dst, ssem, rsem, to):
        return pltpu.make_async_remote_copy(
            src_ref=src, dst_ref=dst, send_sem=ssem, recv_sem=rsem, device_id=to, device_id_type=MESH
        )

    def to_tm(buf, ssem, rsem):
        copies = []
        for k in range(1, tm):
            c = remote(buf.at[t], buf.at[t], ssem.at[k - 1], rsem.at[k - 1], (me, (t + k) % tm))
            c.start()
            copies.append(c)
        return copies

    for it in range(ITERS):
        last = it == ITERS - 1
        sends = []

        def cast(i, _):
            at = pl.ds(pl.multiple_of(i * blk, blk), blk)
            x = u[at, :]
            ub[at, :] = x.astype(BF16)
            ubt[:, at] = x.T.astype(BF16)
            return 0

        lax.fori_loop(0, rows // blk, cast, 0)
        vb[...] = v[...].astype(BF16)
        gram_v[it, t] = dot(v[...].T.astype(BF16), vb[...])
        grams = to_tm(gram_v.at[it], s_gram.at[it], r_gram.at[it])
        sends += grams

        acc[...] = jnp.zeros_like(acc)
        step = 256

        def residual(i, _):
            at = pl.ds(pl.multiple_of(i * step, step), step)
            d = data[at, :].astype(F32) - dot_nt(ub[at, :], vb[...])
            diff[at, :] = d
            acc[...] += jnp.sum(jnp.abs(d).reshape(step // 8, 8, cols), axis=0)
            return 0

        lax.fori_loop(0, rows // step, residual, 0)
        part = acc[:, 0:128]
        for j in range(1, cols // 128):
            part = part + acc[:, j * 128:(j + 1) * 128]
        tot_tm[it, t] = part
        firsts = to_tm(tot_tm.at[it], s_tot_tm.at[it], r_tot_tm.at[it])
        sends += firsts
        for c in firsts:
            c.wait_recv()
        tot_sp[it, me] = jnp.sum(tot_tm[it], axis=0)
        seconds = []
        for k in range(1, n):
            c = remote(
                tot_sp.at[it, me], tot_sp.at[it, me], s_tot_sp.at[it, k - 1], r_tot_sp.at[it, k - 1],
                ((me + k) % n, t),
            )
            c.start()
            seconds.append(c)
        sends += seconds

        gram = dot(ubt[...], ub[...])
        for gg in range(G):
            for hh in range(H):
                r0 = (gg * H + hh) * gr
                pay[it, gg, hh, vr:vr + gr] = gram[r0:r0 + gr]
        for c in seconds:
            c.wait_recv()
        lam = threshold_scale * total_of(jnp.sum(tot_sp[it], axis=0)) / count

        for s in list(range(1, G)) + [0]:
            gg = g ^ s
            c0 = pl.ds(pl.multiple_of(gg * width, width), width)
            gradt[...] = jnp.zeros_like(gradt)

            def gradient(i, _, c0=c0, first=(s == 1 or G == 1)):
                at = pl.ds(pl.multiple_of(i * blk, blk), blk)
                d = diff[at, c0]
                sp = (d - jnp.minimum(jnp.maximum(d, -lam), lam)).astype(BF16)
                if last:
                    sparse[at, c0] = sp
                e = (sp.astype(F32) - d).astype(BF16)
                gu = dot(e, vb[c0, :])
                if first:
                    rows_sum[it, t, at, :] = gu
                else:
                    rows_sum[it, t, at, :] += gu
                gradt[...] += dot(ubt[:, at], e)
                return 0

            lax.fori_loop(0, rows // blk, gradient, 0)
            gv = gradt[...].T
            for hh in range(H):
                pay[it, gg, hh, 0:vr] = gv[hh * vr:(hh + 1) * vr]
            if s:
                c = remote(
                    pay.at[it, gg], plane_in.at[it, s - 1], s_plane.at[it, s - 1], r_plane.at[it, s - 1],
                    (h * G + gg, t),
                )
                c.start()
                sends.append(c)
        row_copies = to_tm(rows_sum.at[it], s_rows.at[it], r_rows.at[it])
        sends += row_copies

        for s in range(1, G):
            remote(
                pay.at[it, g], plane_in.at[it, s - 1], s_plane.at[it, s - 1], r_plane.at[it, s - 1], (h * G + (g ^ s), t)
            ).wait_recv()
        whole = pay[it, g]
        for s in range(1, G):
            whole = whole + plane_in[it, s - 1]
        zsum[it] = whole
        zc = []
        for k in range(1, H):
            to = (h + k) % H
            c = remote(
                zsum.at[it, to], z_in.at[it, k - 1], s_z.at[it, k - 1], r_z.at[it, k - 1], (to * G + g, t)
            )
            c.start()
            zc.append(c)
        sends += zc
        for c in grams:
            c.wait_recv()
        gsum = jnp.sum(gram_v[it], axis=0)
        eta_u = step_scale / jnp.sqrt(total_of(gsum * gsum))
        for c in zc:
            c.wait_recv()
        mine = zsum[it, h]
        for k in range(1, H):
            mine = mine + z_in[it, k - 1]
        gathered[it, g, h] = mine

        def to_plane(k, src_h):
            out = []
            for s in range(1, G):
                c = remote(
                    gathered.at[it, g, src_h], gathered.at[it, g, src_h],
                    s_pg.at[it, k, s - 1], r_pg.at[it, k, s - 1], (h * G + (g ^ s), t),
                )
                c.start()
                out.append(c)
            return out

        zg = []
        for k in range(1, H):
            to = (h + k) % H
            c = remote(
                gathered.at[it, g, h], gathered.at[it, g, h], s_zg.at[it, k - 1], r_zg.at[it, k - 1], (to * G + g, t)
            )
            c.start()
            zg.append(c)
        pg = to_plane(0, h)
        for k in range(1, H):
            zg[k - 1].wait_recv()
            pg += to_plane(k, (h + H - k) % H)
        sends += zg + pg

        for c in row_copies:
            c.wait_recv()

        def step_u(i, _):
            at = pl.ds(pl.multiple_of(i * blk, blk), blk)
            x = u[at, :]
            gu = rows_sum[it, 0, at, :]
            for k in range(1, tm):
                gu = gu + rows_sum[it, k, at, :]
            u[at, :] = x - eta_u * (gu + ridge_weight * x)
            return 0

        lax.fori_loop(0, rows // blk, step_u, 0)
        for c in pg:
            c.wait_recv()
        squares = jnp.zeros((gr, rank), F32)
        for gg in range(G):
            for hh in range(H):
                x = gathered[it, gg, hh, vr:vr + gr]
                squares = squares + x * x
        eta_v = step_scale / jnp.sqrt(total_of(squares))
        for gg in range(G):
            for hh in range(H):
                at = pl.ds((gg * H + hh) * vr, vr)
                x = v[at, :]
                v[at, :] = x - eta_v * (gathered[it, gg, hh, 0:vr] + ridge_weight * x)
        for c in sends:
            c.wait_send()


def solution(mesh):
    n, tm = mesh.shape["space"], mesh.shape["tm"]
    G = 4 if n % 4 == 0 else (2 if n % 2 == 0 else 1)
    H = n // G

    def body(data, row_factor, col_factor):
        rows, cols = data.shape
        rank = row_factor.shape[1]
        width = cols // G
        vr, gr = width // H, rank // n
        R = vr + gr
        count = float(rows * n * cols * tm)

        def sems(*shape):
            return [pltpu.SemaphoreType.DMA((ITERS,) + tuple(max(x, 1) for x in shape))] * 2

        vm = pl.BlockSpec(memory_space=pltpu.VMEM)
        return pl.pallas_call(
            functools.partial(kernel, n, tm, G, H, count),
            out_shape=(
                jax.ShapeDtypeStruct((rows, cols), BF16),
                jax.ShapeDtypeStruct(row_factor.shape, F32),
                jax.ShapeDtypeStruct(col_factor.shape, F32),
            ),
            in_specs=[vm] * 3,
            out_specs=(vm, vm, vm),
            scratch_shapes=[
                pltpu.VMEM((rows, cols), F32),
                pltpu.VMEM((rows, rank), BF16),
                pltpu.VMEM((rank, rows), BF16),
                pltpu.VMEM((cols, rank), BF16),
                pltpu.VMEM((8, cols), F32),
                pltpu.VMEM((rank, width), F32),
                pltpu.VMEM((ITERS, tm, 8, 128), F32),
                pltpu.VMEM((ITERS, n, 8, 128), F32),
                pltpu.VMEM((ITERS, tm, rank, rank), F32),
                pltpu.VMEM((ITERS, tm, rows, rank), F32),
                pltpu.VMEM((ITERS, G, H, R, rank), F32),
                pltpu.VMEM((ITERS, max(G - 1, 1), H, R, rank), F32),
                pltpu.VMEM((ITERS, H, R, rank), F32),
                pltpu.VMEM((ITERS, max(H - 1, 1), R, rank), F32),
                pltpu.VMEM((ITERS, G, H, R, rank), F32),
            ]
            + sems(tm - 1) + sems(n - 1) + sems(tm - 1) + sems(tm - 1)
            + sems(G - 1) + sems(H - 1) + sems(H - 1) + sems(H, G - 1),
            compiler_params=pltpu.CompilerParams(
                collective_id=0, has_side_effects=True, vmem_limit_bytes=58 * 1024 * 1024
            ),
        )(data, row_factor, col_factor)

    return jax.shard_map(
        body,
        mesh=mesh,
        in_specs=(P("space", "tm"), P("space", None), P("tm", None)),
        out_specs=(P("space", "tm"), P("space", None), P("tm", None)),
        check_vma=False,
    )
```

```python
import functools

import jax
import jax.numpy as jnp
from jax import lax
from jax.experimental import pallas as pl
from jax.experimental.pallas import tpu as pltpu
from jax.sharding import PartitionSpec as P

ITERS = 2
MESH = pl.DeviceIdType.MESH
F32 = jnp.float32
BF16 = jnp.bfloat16

threshold_scale = 1.0
step_scale = 8.0
ridge_weight = 64.0


def dot(a, b):
    return jnp.dot(a, b, preferred_element_type=F32)


def dot_nt(a, b):
    return lax.dot_general(a, b, (((1,), (1,)), ((), ())), preferred_element_type=F32)


def total_of(x):
    return jnp.sum(jnp.sum(x, axis=0, keepdims=True), axis=1, keepdims=True)


def kernel(
    n, tm, G, H, count,
    data_in, u_in, v_in, sparse_out, u_out, v_out,
    data, sparse, u, v, diff, ub, ubt, vb, acc, gradt, tot_tm, tot_sp, gram_v, rows_sum, pay, gpiece, plane_in, zsum, z_in, gathered,
    s_tot_tm, r_tot_tm, s_tot_sp, r_tot_sp, s_gram, r_gram, s_rows, r_rows,
    s_plane, r_plane, s_z, r_z, s_zg, r_zg, s_pg, r_pg, in_sem, out_sem,
):
    me = lax.axis_index("space")
    t = lax.axis_index("tm")
    h, g = me // G, me % G
    rows, cols = data.shape
    rank = u.shape[1]
    width = cols // G
    vr = width // H
    gr = rank // n
    blk = min(512, rows)

    barrier = pltpu.get_barrier_semaphore()
    for k in range(1, n):
        pl.semaphore_signal(barrier, inc=1, device_id=((me + k) % n, t), device_id_type=MESH)
    for k in range(1, tm):
        pl.semaphore_signal(barrier, inc=1, device_id=(me, (t + k) % tm), device_id_type=MESH)
    step = 256
    load_v = pltpu.make_async_copy(v_in, v, in_sem.at[0])
    load_u = pltpu.make_async_copy(u_in, u, in_sem.at[1])
    load_v.start()
    load_u.start()

    def load(i):
        at = pl.ds(pl.multiple_of(i * step, step), step)
        return pltpu.make_async_copy(data_in.at[at, :], data.at[at, :], in_sem.at[2 + i])

    for i in range(rows // step):
        load(i).start()
    load_v.wait()
    load_u.wait()

    def remote(src, dst, ssem, rsem, to):
        return pltpu.make_async_remote_copy(
            src_ref=src, dst_ref=dst, send_sem=ssem, recv_sem=rsem, device_id=to, device_id_type=MESH
        )

    def to_tm(buf, ssem, rsem):
        copies = []
        for k in range(1, tm):
            c = remote(buf.at[t], buf.at[t], ssem.at[k - 1], rsem.at[k - 1], (me, (t + k) % tm))
            c.start()
            copies.append(c)
        return copies

    def cast(i, _):
        at = pl.ds(pl.multiple_of(i * blk, blk), blk)
        x = u[at, :]
        ub[at, :] = x.astype(BF16)
        ubt[:, at] = x.T.astype(BF16)
        return 0

    def row_gram(it):
        gram = dot(ubt[...], ub[...])
        for p in range(n):
            gpiece[it, p, 8:8 + gr] = gram[p * gr:(p + 1) * gr]

    lax.fori_loop(0, rows // blk, cast, 0)
    row_gram(0)
    stores = []

    for it in range(ITERS):
        last = it == ITERS - 1
        sends = []
        vb[...] = v[...].astype(BF16)

        acc[...] = jnp.zeros_like(acc)

        def residual(i, _):
            if it == 0:
                load(i).wait()
            at = pl.ds(pl.multiple_of(i * step, step), step)
            d = data[at, :].astype(F32) - dot_nt(ub[at, :], vb[...])
            diff[at, :] = d
            acc[...] += jnp.sum(jnp.abs(d).reshape(step // 8, 8, cols), axis=0)
            return 0

        lax.fori_loop(0, rows // step, residual, 0)
        part = acc[:, 0:128]
        for j in range(1, cols // 128):
            part = part + acc[:, j * 128:(j + 1) * 128]
        tot_tm[it, t] = part
        if it == 0:
            pl.semaphore_wait(barrier, n - 1 + tm - 1)
        firsts = to_tm(tot_tm.at[it], s_tot_tm.at[it], r_tot_tm.at[it])
        sends += firsts
        gram_v[it, t] = dot(v[...].T.astype(BF16), vb[...])
        for c in firsts:
            c.wait_recv()
        part = jnp.sum(tot_tm[it], axis=0)
        for p in range(n):
            gpiece[it, p, 0:8] = part
        tot_sp[it, me] = gpiece[it, me]
        seconds = []
        for k in range(1, n):
            to = (me + k) % n
            c = remote(
                gpiece.at[it, to], tot_sp.at[it, me], s_tot_sp.at[it, k - 1], r_tot_sp.at[it, k - 1], (to, t)
            )
            c.start()
            seconds.append(c)
        grams = to_tm(gram_v.at[it], s_gram.at[it], r_gram.at[it])
        sends += seconds + grams
        for c in seconds:
            c.wait_recv()
        sums = jnp.sum(tot_sp[it], axis=0)
        lam = threshold_scale * total_of(sums[0:8]) / count
        gram = sums[8:8 + gr]
        gathered[it, g, h, vr:vr + gr] = gram * gram

        for s in list(range(G - 1, 0, -1)) + [0]:
            gg = g ^ s
            c0 = pl.ds(pl.multiple_of(gg * width, width), width)
            gradt[...] = jnp.zeros_like(gradt)

            def gradient(i, _, c0=c0, first=(s == G - 1)):
                at = pl.ds(pl.multiple_of(i * blk, blk), blk)
                d = diff[at, c0]
                sp = (d - jnp.minimum(jnp.maximum(d, -lam), lam)).astype(BF16)
                if last:
                    sparse[at, c0] = sp
                e = (sp.astype(F32) - d).astype(BF16)
                gu = dot(e, vb[c0, :])
                if first:
                    rows_sum[it, t, at, :] = gu
                else:
                    rows_sum[it, t, at, :] += gu
                gradt[...] += dot(ubt[:, at], e)
                return 0

            lax.fori_loop(0, rows // blk, gradient, 0)
            gv = gradt[...].T
            for hh in range(H):
                pay[it, gg, hh, 0:vr] = gv[hh * vr:(hh + 1) * vr]
            if last:
                c = pltpu.make_async_copy(sparse.at[:, c0], sparse_out.at[:, c0], out_sem.at[s])
                c.start()
                stores.append(c)
            if s:
                c = remote(
                    pay.at[it, gg], plane_in.at[it, s - 1], s_plane.at[it, s - 1], r_plane.at[it, s - 1],
                    (h * G + gg, t),
                )
                c.start()
                sends.append(c)
        row_copies = to_tm(rows_sum.at[it], s_rows.at[it], r_rows.at[it])
        sends += row_copies

        for s in range(1, G):
            remote(
                pay.at[it, g], plane_in.at[it, s - 1], s_plane.at[it, s - 1], r_plane.at[it, s - 1], (h * G + (g ^ s), t)
            ).wait_recv()
        whole = pay[it, g]
        for s in range(1, G):
            whole = whole + plane_in[it, s - 1]
        zsum[it] = whole
        zc = []
        for k in range(1, H):
            to = (h + k) % H
            c = remote(
                zsum.at[it, to], z_in.at[it, k - 1], s_z.at[it, k - 1], r_z.at[it, k - 1], (to * G + g, t)
            )
            c.start()
            zc.append(c)
        sends += zc
        for c in grams:
            c.wait_recv()
        gsum = jnp.sum(gram_v[it], axis=0)
        eta_u = step_scale / jnp.sqrt(total_of(gsum * gsum))
        for c in zc:
            c.wait_recv()
        mine = zsum[it, h]
        for k in range(1, H):
            mine = mine + z_in[it, k - 1]
        gathered[it, g, h, 0:vr] = mine

        def to_plane(k, src_h):
            out = []
            for s in range(1, G):
                c = remote(
                    gathered.at[it, g, src_h], gathered.at[it, g, src_h],
                    s_pg.at[it, k, s - 1], r_pg.at[it, k, s - 1], (h * G + (g ^ s), t),
                )
                c.start()
                out.append(c)
            return out

        zg = []
        for k in range(1, H):
            to = (h + k) % H
            c = remote(
                gathered.at[it, g, h], gathered.at[it, g, h], s_zg.at[it, k - 1], r_zg.at[it, k - 1], (to * G + g, t)
            )
            c.start()
            zg.append(c)
        pg = to_plane(0, h)
        for k in range(1, H):
            zg[k - 1].wait_recv()
            pg += to_plane(k, (h + H - k) % H)
        sends += zg + pg

        for c in row_copies:
            c.wait_recv()

        def step_u(i, _):
            at = pl.ds(pl.multiple_of(i * blk, blk), blk)
            x = u[at, :]
            gu = rows_sum[it, 0, at, :]
            for k in range(1, tm):
                gu = gu + rows_sum[it, k, at, :]
            u[at, :] = x - eta_u * (gu + ridge_weight * x)
            return 0

        lax.fori_loop(0, rows // blk, step_u, 0)
        if last:
            c = pltpu.make_async_copy(u, u_out, out_sem.at[G])
            c.start()
            stores.append(c)
        else:
            lax.fori_loop(0, rows // blk, cast, 0)
            row_gram(it + 1)
        for c in pg:
            c.wait_recv()
        squares = jnp.zeros((gr, rank), F32)
        for gg in range(G):
            for hh in range(H):
                squares = squares + gathered[it, gg, hh, vr:vr + gr]
        eta_v = step_scale / jnp.sqrt(total_of(squares))
        for gg in range(G):
            for hh in range(H):
                at = pl.ds((gg * H + hh) * vr, vr)
                x = v[at, :]
                v[at, :] = x - eta_v * (gathered[it, gg, hh, 0:vr] + ridge_weight * x)
        for c in sends:
            c.wait_send()
    c = pltpu.make_async_copy(v, v_out, out_sem.at[G + 1])
    c.start()
    for c in stores + [c]:
        c.wait()


def solution(mesh):
    n, tm = mesh.shape["space"], mesh.shape["tm"]
    G = 4 if n % 4 == 0 else (2 if n % 2 == 0 else 1)
    H = n // G

    def body(data, row_factor, col_factor):
        rows, cols = data.shape
        rank = row_factor.shape[1]
        width = cols // G
        vr, gr = width // H, rank // n
        R = vr + gr
        count = float(rows * n * cols * tm)

        def sems(*shape):
            return [pltpu.SemaphoreType.DMA((ITERS,) + tuple(max(x, 1) for x in shape))] * 2

        vm = pl.BlockSpec(memory_space=pl.ANY)
        shapes = (
            jax.ShapeDtypeStruct((rows, cols), BF16),
            jax.ShapeDtypeStruct(row_factor.shape, F32),
            jax.ShapeDtypeStruct(col_factor.shape, F32),
        )
        held = pl.pallas_call(
            functools.partial(kernel, n, tm, G, H, count),
            out_shape=shapes,
            in_specs=[vm] * 3,
            out_specs=(vm, vm, vm),
            scratch_shapes=[
                pltpu.VMEM((rows, cols), BF16),
                pltpu.VMEM((rows, cols), BF16),
                pltpu.VMEM((rows, rank), F32),
                pltpu.VMEM((cols, rank), F32),
                pltpu.VMEM((rows, cols), F32),
                pltpu.VMEM((rows, rank), BF16),
                pltpu.VMEM((rank, rows), BF16),
                pltpu.VMEM((cols, rank), BF16),
                pltpu.VMEM((8, cols), F32),
                pltpu.VMEM((rank, width), F32),
                pltpu.VMEM((ITERS, tm, 8, 128), F32),
                pltpu.VMEM((ITERS, n, 8 + gr, 128), F32),
                pltpu.VMEM((ITERS, tm, rank, rank), F32),
                pltpu.VMEM((ITERS, tm, rows, rank), F32),
                pltpu.VMEM((ITERS, G, H, vr, rank), F32),
                pltpu.VMEM((ITERS, n, 8 + gr, 128), F32),
                pltpu.VMEM((ITERS, max(G - 1, 1), H, vr, rank), F32),
                pltpu.VMEM((ITERS, H, vr, rank), F32),
                pltpu.VMEM((ITERS, max(H - 1, 1), vr, rank), F32),
                pltpu.VMEM((ITERS, G, H, R, rank), F32),
            ]
            + sems(tm - 1) + sems(n - 1) + sems(tm - 1) + sems(tm - 1)
            + sems(G - 1) + sems(H - 1) + sems(H - 1) + sems(H, G - 1)
            + [pltpu.SemaphoreType.DMA((2 + rows // 256,)), pltpu.SemaphoreType.DMA((G + 2,))],
            compiler_params=pltpu.CompilerParams(
                collective_id=0, has_side_effects=True, vmem_limit_bytes=58 * 1024 * 1024
            ),
        )(data, row_factor, col_factor)
        return held

    return jax.shard_map(
        body,
        mesh=mesh,
        in_specs=(P("space", "tm"), P("space", None), P("tm", None)),
        out_specs=(P("space", "tm"), P("space", None), P("tm", None)),
        check_vma=False,
    )
```
